32 devices in a mesh: ctx: 16 (over z, y, x), head: 2 (over core).
Axes of the slice: x: 2, y: 2, z: 4, core: 2. Of those that a mesh axis runs over, the one named last changes fastest.
Arguments:
- space_head_input: bfloat16 [8192, 6144], P('ctx', 'head'), may hold values from -6 to 6
- mixer_gate_input: bfloat16 [8192, 6144], P('ctx', 'head'), may hold values from -12 to 12
- state_write_matrix: bfloat16 [8192, 128], P('ctx'), may hold values from -1.78125 to 1.78125
- readout_matrix: bfloat16 [8192, 128], P('ctx'), may hold values from -1.78125 to 1.78125
- head_decay_code: int32 [24], P('head'), may hold values from 0 to 7
- token_step_code: int32 [24, 8192], P('head', 'ctx'), may hold values from 0 to 3
- forget_token_code: int32 [8192], P('ctx'), may hold values from 0 to 3, as said below
- head_direct_gain: float32 [24], P('head'), may hold values from 0.5 to 1.5
- output_norm_gain: float32 [6144], P('head'), may hold values from 0.5 to 1.5
- attention_query: bfloat16 [8192, 3072], P('ctx', 'head'), may hold values from -6.5 to 6.5
- attention_key: bfloat16 [8192, 3072], P('ctx', 'head'), may hold values from -6.5 to 6.5
- attention_value: bfloat16 [8192, 3072], P('ctx', 'head'), may hold values from -6 to 6
Outputs:
- mixer_out: bfloat16 [8192, 6144], P('ctx', 'head')
- window_out: bfloat16 [8192, 3072], P('ctx', 'head')
The draws below stay inside these ranges and needn't reach their ends.
Inputs may be any that keep to these rules, and one draw needn't show every extreme that they name: `forget_token_code`: at most four tokens have a nonzero code; one has 3.
All inputs are finite; a program needn't handle non-finite values.
Results may differ from the reference program's by a relative error of at most 0.0043.
Values may be sent and summed in bfloat16 or wider, within the bound.
A program may use at most 256 MiB of HBM per device.

```python
import math
import jax
import jax.numpy as jnp
from jax import lax

HEADS = 24
HD = 128
SSM_HEADS = 24
P_SIZE = 256
N = 128
WINDOW = 2048
BLOCK = 256
TOK_DEV = 512
TOKEN_COUNT = 8192


def draw_forget_token_code(key, part):
    forget_rows = jax.random.randint(jax.random.fold_in(key, 31), (4,), 0, TOKEN_COUNT)
    level_count = jax.random.randint(jax.random.fold_in(key, 32), (4,), 1, 4)
    level_count = level_count.at[0].set(3)
    return jnp.zeros((TOKEN_COUNT,), jnp.int32).at[forget_rows].max(level_count)


def draw_mixer_gate_input(key, part):
    columns = SSM_HEADS * P_SIZE
    column_ramp = jnp.exp(jnp.log(3.0) * jnp.arange(columns, dtype=jnp.float32) / columns)
    base_draw = jnp.clip(jax.random.normal(jax.random.fold_in(key, 41), (TOKEN_COUNT, columns), jnp.float32), -4.0, 4.0)
    return (base_draw * column_ramp[None, :]).astype(jnp.bfloat16)


def draw_attention_query(key, part):
    columns = HEADS * HD
    base_draw = jnp.clip(jax.random.normal(jax.random.fold_in(key, 21), (TOKEN_COUNT, columns), jnp.float32), -4.0, 4.0)
    return base_draw.astype(jnp.bfloat16)


def draw_attention_key(key, part):
    columns = HEADS * HD
    base_draw = jnp.clip(jax.random.normal(jax.random.fold_in(key, 22), (TOKEN_COUNT, columns), jnp.float32), -4.0, 4.0)
    return base_draw.astype(jnp.bfloat16)


def with_ends(array, stream_key, smallest, largest):
    index_at = [jax.random.randint(jax.random.fold_in(stream_key, axis), (), 0, length) for axis, length in enumerate(array.shape)]
    longest = array.shape.index(max(array.shape))
    beside = index_at[:longest] + [(index_at[longest] + 1) % array.shape[longest]] + index_at[longest + 1:]
    return array.at[tuple(index_at)].set(smallest).at[tuple(beside)].set(largest)


def shard_levels(key, dims, cuts, least, largest):
    factor_of = 1.0
    for position, parts in cuts:
        heights = jax.random.uniform(jax.random.fold_in(jax.random.fold_in(key, 6), position), (parts,), jnp.float32, least / len(cuts), largest / len(cuts))
        factor_of = factor_of * jnp.repeat(jnp.exp(heights), dims[position] // parts).reshape((-1,) + (1,) * (len(dims) - 1 - position))
    return factor_of


def normal_values(stream_key, shape, spread, reach, shards=(), kind=jnp.bfloat16):
    drawn = jax.random.normal(stream_key, shape, jnp.float32) * spread
    if len(shards) > 0:
        drawn = shard_levels(stream_key, shape, shards, -0.22, 0.18) * drawn
    return jnp.clip(drawn, min=-reach, max=reach).astype(kind)


def setup_inputs(seed: int = 0) -> dict:
    splits = jax.random.split(jax.random.key(seed), 13)
    space_head_input = normal_values(splits[0], (TOKEN_COUNT, SSM_HEADS * P_SIZE), 1.0, 6.0, ((0, 16), (1, 2)))
    mixer_gate_input = draw_mixer_gate_input(jax.random.fold_in(splits[12], 71), 0)
    state_write_matrix = normal_values(splits[2], (TOKEN_COUNT, N), (N ** -0.25), 1.78125, ((0, 16),))
    readout_matrix = normal_values(splits[3], (TOKEN_COUNT, N), (N ** -0.25), 1.78125, ((0, 16),))
    head_decay_code = with_ends(jax.random.randint(splits[4], (SSM_HEADS,), 0, 8), jax.random.fold_in(splits[4], 1), 0, 7).astype(jnp.int32)
    token_step_code = with_ends(jax.random.randint(splits[5], (SSM_HEADS, TOKEN_COUNT), 0, 4), jax.random.fold_in(splits[5], 1), 0, 3).astype(jnp.int32)
    forget_token_code = draw_forget_token_code(jax.random.fold_in(splits[12], 71), 0)
    head_direct_gain = jnp.clip(0.5 + 1.0 * jax.random.uniform(splits[7], (SSM_HEADS,), jnp.float32) ** shard_levels(splits[7], (SSM_HEADS,), ((0, 2),), -0.2, 0.2), 0.5, 1.5)
    output_norm_gain = jnp.clip(0.5 + 1.0 * jax.random.uniform(splits[8], (SSM_HEADS * P_SIZE,), jnp.float32) ** shard_levels(splits[8], (SSM_HEADS * P_SIZE,), ((0, 2),), -0.2, 0.2), 0.5, 1.5)
    attention_query = draw_attention_query(jax.random.fold_in(splits[12], 71), 0)
    attention_key = draw_attention_key(jax.random.fold_in(splits[12], 71), 0)
    attention_value = normal_values(splits[11], (TOKEN_COUNT, HEADS * HD), 1.0, 6.0, ((0, 16), (1, 2)))
    return dict(space_head_input=space_head_input, mixer_gate_input=mixer_gate_input, state_write_matrix=state_write_matrix, readout_matrix=readout_matrix, head_decay_code=head_decay_code, token_step_code=token_step_code, forget_token_code=forget_token_code, head_direct_gain=head_direct_gain, output_norm_gain=output_norm_gain, attention_query=attention_query, attention_key=attention_key, attention_value=attention_value)


def head_rates(head_decay_code, token_total_count):
    level_count = head_decay_code.astype(jnp.float32)
    quick_log = math.log(0.03) - level_count / 4.0 * math.log(0.03 * token_total_count)
    gentle = -math.log(token_total_count) - (level_count - 4.0) / 3.0 * math.log(4.0)
    return jnp.exp(jnp.where(level_count <= 4.0, quick_log, gentle))

def decay_factors(head_decay_code, token_step_code, forget_token_code, token_total_count):
    every_rate = head_rates(head_decay_code, token_total_count)
    token_step_sizes = jnp.sqrt(2.0 * every_rate)[:, None] * jnp.exp(math.log(2.0) * (0.5 * token_step_code.astype(jnp.float32) - 0.75))
    logarithm_decay = -jnp.sqrt(0.5 * every_rate)[:, None] * token_step_sizes - 0.2 * forget_token_code.astype(jnp.float32)[None, :]
    return (token_step_sizes, logarithm_decay)

def reference(space_head_input, mixer_gate_input, state_write_matrix, readout_matrix, head_decay_code, token_step_code, forget_token_code, head_direct_gain, output_norm_gain, attention_query, attention_key, attention_value):
    highest = lax.Precision.HIGHEST
    token_step_sizes, logarithm_decay = decay_factors(head_decay_code, token_step_code, forget_token_code, TOKEN_COUNT)
    blocks = TOKEN_COUNT // BLOCK
    inputs_block = space_head_input.reshape(blocks, BLOCK, SSM_HEADS, P_SIZE)
    write_block = state_write_matrix.reshape(blocks, BLOCK, N)
    read_block = readout_matrix.reshape(blocks, BLOCK, N)
    sizes_block = jnp.transpose(token_step_sizes.reshape(SSM_HEADS, blocks, BLOCK), (1, 0, 2))
    decay_block = jnp.transpose(logarithm_decay.reshape(SSM_HEADS, blocks, BLOCK), (1, 0, 2))
    lower_mask = jnp.arange(BLOCK)[:, None] >= jnp.arange(BLOCK)[None, :]

    def block_update(carried, pieces):
        inputs_here, write_here, read_here, sizes_here, decay_here = pieces
        cumulative = jnp.cumsum(decay_here, axis=1)
        cross_map = jnp.dot(read_here, write_here.T, preferred_element_type=jnp.float32)
        gap_matrix = cumulative[:, :, None] - cumulative[:, None, :]
        mixing = jnp.where(lower_mask, jnp.exp(jnp.where(lower_mask, gap_matrix, 0.0)) * cross_map[None] * sizes_here[:, None, :], 0.0)
        mixing = lax.optimization_barrier(mixing.astype(jnp.bfloat16)).astype(jnp.float32)
        inputs_wide = inputs_here.astype(jnp.float32)
        intra_part = jnp.einsum('hts,shp->thp', mixing, inputs_wide, precision=highest)
        inter_part = jnp.einsum('tn,hpn->thp', read_here.astype(jnp.float32), carried, precision=highest) * jnp.exp(cumulative).T[:, :, None]
        tail_weights = jnp.exp(cumulative[:, -1:] - cumulative) * sizes_here
        fresh_state = jnp.einsum('shp,hsn->hpn', inputs_wide, tail_weights[:, :, None] * write_here.astype(jnp.float32)[None], precision=highest)
        carried = jnp.exp(cumulative[:, -1])[:, None, None] * carried + fresh_state
        return (carried, intra_part + inter_part)
    start_state = jnp.zeros((SSM_HEADS, P_SIZE, N), jnp.float32)
    _, outputs = lax.scan(block_update, start_state, (inputs_block, write_block, read_block, sizes_block, decay_block))
    mixed_all = outputs.reshape(TOKEN_COUNT, SSM_HEADS, P_SIZE) + head_direct_gain[None, :, None] * space_head_input.reshape(TOKEN_COUNT, SSM_HEADS, P_SIZE).astype(jnp.float32)
    gated_out = mixed_all.reshape(TOKEN_COUNT, SSM_HEADS * P_SIZE) * jax.nn.silu(mixer_gate_input.astype(jnp.float32))
    mean_square = lax.optimization_barrier(jnp.mean(gated_out * gated_out, axis=1, keepdims=True))
    mixer_out = (gated_out * lax.rsqrt(mean_square + 1e-05) * output_norm_gain).astype(jnp.bfloat16)
    score_scale = HD ** (-0.5)
    query_heads = attention_query.reshape(TOKEN_COUNT, HEADS, HD)
    key_padded = jnp.pad(attention_key.reshape(TOKEN_COUNT, HEADS, HD), ((WINDOW, 0), (0, 0), (0, 0)))
    value_padded = jnp.pad(attention_value.reshape(TOKEN_COUNT, HEADS, HD), ((WINDOW, 0), (0, 0), (0, 0)))

    def attend(block_number):
        first_row = block_number * TOK_DEV
        query_here = lax.dynamic_slice_in_dim(query_heads, first_row, TOK_DEV, 0)
        key_here = lax.dynamic_slice_in_dim(key_padded, first_row, WINDOW + TOK_DEV, 0)
        value_here = lax.dynamic_slice_in_dim(value_padded, first_row, WINDOW + TOK_DEV, 0)
        scores = jnp.einsum('qhd,khd->hqk', query_here.astype(jnp.float32), key_here.astype(jnp.float32), precision=highest) * score_scale
        query_pos = first_row + jnp.arange(TOK_DEV, dtype=jnp.int32)
        key_pos = first_row - WINDOW + jnp.arange(WINDOW + TOK_DEV, dtype=jnp.int32)
        in_window = (key_pos[None, :] <= query_pos[:, None]) & (key_pos[None, :] > query_pos[:, None] - WINDOW) & (key_pos[None, :] >= 0)
        scores = jnp.where(in_window[None], scores, -jnp.inf)
        maximum = lax.optimization_barrier(jnp.max(scores, axis=2, keepdims=True))
        weights_f = jnp.exp(scores - maximum)
        row_total = lax.optimization_barrier(jnp.sum(weights_f, axis=2))
        weights_b = lax.optimization_barrier(weights_f.astype(jnp.bfloat16)).astype(jnp.float32)
        attended = jnp.einsum('hqk,khd->qhd', weights_b, value_here.astype(jnp.float32), precision=highest) / row_total.T[:, :, None]
        return attended.astype(jnp.bfloat16).reshape(TOK_DEV, HEADS * HD)
    window_out = lax.map(attend, jnp.arange(TOKEN_COUNT // TOK_DEV, dtype=jnp.int32)).reshape(TOKEN_COUNT, HEADS * HD)
    return (mixer_out, window_out)
```

```python
import functools
import math

import jax
import jax.numpy as jnp
from jax import lax
from jax.experimental import pallas as pl
from jax.experimental.pallas import tpu as pltpu
from jax.sharding import PartitionSpec as P

HD = 128
SSM_HEADS = 24
P_SIZE = 256
WINDOW = 2048
HEAD_GROUPS = 2
VMEM_LIMIT = 48 * 1024 * 1024


def head_rates(head_decay_code, token_total_count):
    level_count = head_decay_code.astype(jnp.float32)
    quick_log = math.log(0.03) - level_count / 4.0 * math.log(0.03 * token_total_count)
    gentle = -math.log(token_total_count) - (level_count - 4.0) / 3.0 * math.log(4.0)
    return jnp.exp(jnp.where(level_count <= 4.0, quick_log, gentle))


def decay_factors(head_decay_code, token_step_code, forget_token_code, token_total_count):
    every_rate = head_rates(head_decay_code, token_total_count)
    token_step_sizes = jnp.sqrt(2.0 * every_rate)[:, None] * jnp.exp(
        math.log(2.0) * (0.5 * token_step_code.astype(jnp.float32) - 0.75)
    )
    logarithm_decay = (
        -jnp.sqrt(0.5 * every_rate)[:, None] * token_step_sizes
        - 0.2 * forget_token_code.astype(jnp.float32)[None, :]
    )
    return (token_step_sizes, logarithm_decay)


def column_of(table, index):
    lanes = lax.broadcasted_iota(jnp.int32, table.shape, 1)
    return jnp.sum(jnp.where(lanes == index, table, 0.0), axis=1, keepdims=True)


def end_state_kernel(x_ref, write_ref, weight_ref, state_ref):
    weight = column_of(weight_ref[...], pl.program_id(0))
    weighted = (write_ref[...].astype(jnp.float32) * weight).astype(jnp.bfloat16)
    state_ref[0] = lax.dot_general(
        weighted, x_ref[...], (((0,), (0,)), ((), ())), preferred_element_type=jnp.float32
    )


def mixer_kernel(
    x_ref, gate_ref, write_ref, read_ref, cum_row_ref, size_row_ref, cum_table_ref, gain_ref,
    incoming_ref, gated_ref, square_ref, cross_ref,
):
    head = pl.program_id(0)
    rows = x_ref.shape[0]
    half = rows // 2

    @pl.when(head == 0)
    def _():
        cross_ref[...] = lax.dot_general(
            read_ref[...], write_ref[...], (((1,), (1,)), ((), ())),
            preferred_element_type=jnp.float32,
        )
        square_ref[...] = jnp.zeros_like(square_ref)

    cum_column = column_of(cum_table_ref[...], head)
    direct = column_of(gain_ref[...], head)
    incoming = incoming_ref[0]
    for part in range(2):
        here = slice(part * half, (part + 1) * half)
        upto = (part + 1) * half
        x_here = x_ref[here, :]
        row_ids = part * half + lax.broadcasted_iota(jnp.int32, (half, upto), 0)
        column_ids = lax.broadcasted_iota(jnp.int32, (half, upto), 1)
        lower = row_ids >= column_ids
        gap = cum_column[here] - cum_row_ref[0, :, :upto]
        mixing = jnp.where(
            lower,
            jnp.exp(jnp.where(lower, gap, 0.0))
            * cross_ref[here, :upto]
            * size_row_ref[0, :, :upto],
            0.0,
        ).astype(jnp.bfloat16)
        mixed = jnp.dot(mixing, x_ref[:upto, :], preferred_element_type=jnp.float32)
        mixed += jnp.exp(cum_column[here]) * jnp.dot(
            read_ref[here, :], incoming, preferred_element_type=jnp.float32
        )
        mixed += direct * x_here.astype(jnp.float32)
        gate = gate_ref[here, :].astype(jnp.float32)
        gated = mixed * (gate / (1.0 + jnp.exp(-gate)))
        gated_ref[here, :] = gated
        square_ref[here, :] += jnp.sum(gated * gated, axis=1, keepdims=True)


def attention_kernel(group, q_ref, *refs):
    key_refs, value_refs, out_ref = refs[: group + 1], refs[group + 1 : -1], refs[-1]
    rows = q_ref.shape[0]
    half = rows // 2
    position = lax.axis_index("ctx")
    mine = position % group
    has_before = position >= group
    scale = HD ** (-0.5)
    for part in range(2):
        query = q_ref[part * half : (part + 1) * half, :]
        spans = [slice(0, (part + 1) * half)]
        spans += [slice(0, rows)] * (group - 1)
        spans += [slice(part * half, rows)]
        all_scores = []
        for which, span in enumerate(spans):
            scores = lax.dot_general(
                query, key_refs[which][span, :], (((1,), (1,)), ((), ())),
                preferred_element_type=jnp.float32,
            )
            if which == 0 or which == group:
                query_ids = part * half + lax.broadcasted_iota(jnp.int32, scores.shape, 0)
                key_ids = span.start + lax.broadcasted_iota(jnp.int32, scores.shape, 1)
                if which == 0:
                    scores = jnp.where(key_ids <= query_ids, scores, -jnp.inf)
                else:
                    kept = jnp.logical_and(key_ids > query_ids, has_before)
                    scores = jnp.where(kept, scores, -jnp.inf)
            else:
                kept = jnp.logical_or(jnp.bitwise_xor(mine, which) < mine, has_before)
                scores = jnp.where(kept, scores, -jnp.inf)
            all_scores.append(scores)
        maximum = functools.reduce(
            jnp.maximum, [jnp.max(scores, axis=1, keepdims=True) for scores in all_scores]
        )
        total = jnp.zeros_like(maximum)
        attended = jnp.zeros((half, HD), jnp.float32)
        for which, span in enumerate(spans):
            weights = jnp.exp((all_scores[which] - maximum) * scale)
            total += jnp.sum(weights, axis=1, keepdims=True)
            attended += jnp.dot(
                weights.astype(jnp.bfloat16), value_refs[which][span, :],
                preferred_element_type=jnp.float32,
            )
        out_ref[part * half : (part + 1) * half, :] = (attended / total).astype(jnp.bfloat16)


def attend(query, pairs, first_head, heads, group):
    rows = query.shape[0]
    block = (rows, HD)
    return pl.pallas_call(
        functools.partial(attention_kernel, group),
        grid=(heads,),
        in_specs=[pl.BlockSpec(block, lambda h: (0, first_head + h))]
        + [pl.BlockSpec(block, lambda h: (0, h))] * (group + 1)
        + [pl.BlockSpec(block, lambda h: (0, heads + h))] * (group + 1),
        out_specs=pl.BlockSpec(block, lambda h: (0, h)),
        out_shape=jax.ShapeDtypeStruct((rows, heads * HD), jnp.bfloat16),
        compiler_params=pltpu.CompilerParams(vmem_limit_bytes=VMEM_LIMIT),
        cost_estimate=pl.CostEstimate(
            flops=4 * heads * rows * rows * (group + 1) * HD,
            bytes_accessed=2 * heads * rows * HD * (2 * group + 4),
            transcendentals=heads * rows * rows * (group + 1),
        ),
    )(query, *pairs, *pairs)


def per_device(
    space_head_input,
    mixer_gate_input,
    state_write_matrix,
    readout_matrix,
    head_decay_code,
    token_step_code,
    forget_token_code,
    head_direct_gain,
    output_norm_gain,
    attention_query,
    attention_key,
    attention_value,
):
    rows = space_head_input.shape[0]
    local_heads = head_decay_code.shape[0]
    state_size = state_write_matrix.shape[1]
    count = lax.axis_size("ctx")
    position = lax.axis_index("ctx")
    group = WINDOW // rows
    mine = position % group
    shift = lambda value, steps: lax.ppermute(
        value, "ctx", [(source, source + steps) for source in range(count - steps)]
    )
    swap = lambda value, bits: lax.ppermute(
        value, "ctx", [(source, source ^ bits) for source in range(count)]
    )

    heads = attention_query.shape[1] // HD
    parts = HEAD_GROUPS if heads % HEAD_GROUPS == 0 else 1
    part_heads = heads // parts
    gathered = []
    for part in range(parts):
        columns = slice(part * part_heads * HD, (part + 1) * part_heads * HD)
        own = jnp.concatenate([attention_key[:, columns], attention_value[:, columns]], axis=1)
        before = shift(own, group)
        sent = {}
        bit = 1
        while bit < group:
            sent[bit] = jnp.where(jnp.bitwise_and(mine, bit) == 0, own, before)
            bit *= 2
        pairs = [own]
        for bits in range(1, group):
            top = 1 << (bits.bit_length() - 1)
            pairs.append(swap(sent[top], bits))
        gathered.append(pairs + [before])

    sizes, log_decay = decay_factors(
        head_decay_code, token_step_code, forget_token_code, rows * count
    )
    upper = (jnp.arange(rows)[:, None] <= jnp.arange(rows)[None, :]).astype(jnp.float32)
    cumulative = jnp.dot(log_decay, upper, precision=lax.Precision.HIGHEST)
    last = cumulative[:, -1]
    logs = lax.all_gather(last, "ctx")
    weights = jnp.exp(last[:, None] - cumulative) * sizes

    state = pl.pallas_call(
        end_state_kernel,
        grid=(local_heads,),
        in_specs=[
            pl.BlockSpec((rows, P_SIZE), lambda h: (0, h)),
            pl.BlockSpec((rows, state_size), lambda h: (0, 0)),
            pl.BlockSpec((rows, local_heads), lambda h: (0, 0)),
        ],
        out_specs=pl.BlockSpec((1, state_size, P_SIZE), lambda h: (h, 0, 0)),
        out_shape=jax.ShapeDtypeStruct((local_heads, state_size, P_SIZE), jnp.float32),
        cost_estimate=pl.CostEstimate(
            flops=2 * local_heads * rows * state_size * P_SIZE,
            bytes_accessed=2 * local_heads * rows * P_SIZE,
            transcendentals=0,
        ),
    )(space_head_input, state_write_matrix, weights.T)

    device_ids = jnp.arange(count)

    def decay_over(first, stop):
        inside = (device_ids >= first) & (device_ids < stop)
        return jnp.exp(jnp.sum(jnp.where(inside[:, None], logs, 0.0), axis=0))[:, None, None]

    prefix = jnp.zeros_like(state)
    total = state
    bit = 1
    while bit < group:
        other = swap(total.astype(jnp.bfloat16), bit).astype(jnp.float32)
        start = position - position % bit
        later = jnp.bitwise_and(position, bit) != 0
        partner = jnp.bitwise_xor(start, bit)
        prefix = jnp.where(later, prefix + decay_over(start, position) * other, prefix)
        total = jnp.where(
            later,
            total + decay_over(start, start + bit) * other,
            other + decay_over(partner, partner + bit) * total,
        )
        bit *= 2
    group_start = position - mine
    earlier = shift(total.astype(jnp.bfloat16), group).astype(jnp.float32)
    span = 1
    while span * group < count - group:
        more = shift(earlier.astype(jnp.bfloat16), span * group).astype(jnp.float32)
        earlier = earlier + decay_over(group_start - span * group, group_start) * more
        span *= 2
    incoming = (prefix + decay_over(group_start, position) * earlier).astype(jnp.bfloat16)

    gated, squares = pl.pallas_call(
        mixer_kernel,
        grid=(local_heads,),
        in_specs=[
            pl.BlockSpec((rows, P_SIZE), lambda h: (0, h)),
            pl.BlockSpec((rows, P_SIZE), lambda h: (0, h)),
            pl.BlockSpec((rows, state_size), lambda h: (0, 0)),
            pl.BlockSpec((rows, state_size), lambda h: (0, 0)),
            pl.BlockSpec((1, 1, rows), lambda h: (h, 0, 0)),
            pl.BlockSpec((1, 1, rows), lambda h: (h, 0, 0)),
            pl.BlockSpec((rows, local_heads), lambda h: (0, 0)),
            pl.BlockSpec((1, local_heads), lambda h: (0, 0)),
            pl.BlockSpec((1, state_size, P_SIZE), lambda h: (h, 0, 0)),
        ],
        out_specs=[
            pl.BlockSpec((rows, P_SIZE), lambda h: (0, h)),
            pl.BlockSpec((rows, 1), lambda h: (0, 0)),
        ],
        out_shape=[
            jax.ShapeDtypeStruct((rows, local_heads * P_SIZE), jnp.float32),
            jax.ShapeDtypeStruct((rows, 1), jnp.float32),
        ],
        scratch_shapes=[pltpu.VMEM((rows, rows), jnp.float32)],
        compiler_params=pltpu.CompilerParams(vmem_limit_bytes=VMEM_LIMIT),
        cost_estimate=pl.CostEstimate(
            flops=2 * local_heads * rows * (rows + state_size) * P_SIZE,
            bytes_accessed=8 * local_heads * rows * P_SIZE,
            transcendentals=local_heads * rows * (rows + P_SIZE),
        ),
    )(
        space_head_input,
        mixer_gate_input,
        state_write_matrix,
        readout_matrix,
        cumulative[:, None, :],
        sizes[:, None, :],
        cumulative.T,
        head_direct_gain[None, :],
        incoming,
    )
    squares = lax.psum(squares[:, 0], "head")
    mixer_out = (
        gated * lax.rsqrt(squares[:, None] / (SSM_HEADS * P_SIZE) + 1e-05) * output_norm_gain
    ).astype(jnp.bfloat16)

    outs = [
        attend(attention_query, gathered[part], part * part_heads, part_heads, group)
        for part in range(parts)
    ]
    window_out = outs[0] if parts == 1 else jnp.concatenate(outs, axis=1)
    return (mixer_out, window_out)


def solution(mesh):
    return jax.shard_map(
        per_device,
        mesh=mesh,
        in_specs=(
            P("ctx", "head"),
            P("ctx", "head"),
            P("ctx", None),
            P("ctx", None),
            P("head"),
            P("head", "ctx"),
            P("ctx"),
            P("head"),
            P("head"),
            P("ctx", "head"),
            P("ctx", "head"),
            P("ctx", "head"),
        ),
        out_specs=(P("ctx", "head"), P("ctx", "head")),
        check_vma=False,
    )
```

```python
import functools
import math

import jax
import jax.numpy as jnp
from jax import lax
from jax.experimental import pallas as pl
from jax.experimental.pallas import tpu as pltpu
from jax.sharding import PartitionSpec as P

HD = 128
SSM_HEADS = 24
P_SIZE = 256
WINDOW = 2048
HEAD_GROUPS = 2
LOG_ROWS = 16
VMEM_LIMIT = 48 * 1024 * 1024


def head_rates(head_decay_code, token_total_count):
    level_count = head_decay_code.astype(jnp.float32)
    quick_log = math.log(0.03) - level_count / 4.0 * math.log(0.03 * token_total_count)
    gentle = -math.log(token_total_count) - (level_count - 4.0) / 3.0 * math.log(4.0)
    return jnp.exp(jnp.where(level_count <= 4.0, quick_log, gentle))


def decay_factors(head_decay_code, token_step_code, forget_token_code, token_total_count):
    every_rate = head_rates(head_decay_code, token_total_count)
    token_step_sizes = jnp.sqrt(2.0 * every_rate)[:, None] * jnp.exp(
        math.log(2.0) * (0.5 * token_step_code.astype(jnp.float32) - 0.75)
    )
    logarithm_decay = (
        -jnp.sqrt(0.5 * every_rate)[:, None] * token_step_sizes
        - 0.2 * forget_token_code.astype(jnp.float32)[None, :]
    )
    return (token_step_sizes, logarithm_decay)


def column_of(table, index):
    lanes = lax.broadcasted_iota(jnp.int32, table.shape, 1)
    return jnp.sum(jnp.where(lanes == index, table, 0.0), axis=1, keepdims=True)


def end_state_kernel(x_ref, write_ref, weight_ref, state_ref):
    weight = column_of(weight_ref[...], pl.program_id(0))
    weighted = (write_ref[...].astype(jnp.float32) * weight).astype(jnp.bfloat16)
    state_ref[0] = lax.dot_general(
        weighted, x_ref[...], (((0,), (0,)), ((), ())), preferred_element_type=jnp.float32
    )


def mixer_kernel(
    x_ref, gate_ref, write_ref, read_ref, cum_row_ref, size_row_ref, cum_table_ref, gain_ref,
    incoming_ref, gated_ref, square_ref, cross_ref,
):
    head = pl.program_id(0)
    rows = x_ref.shape[0]
    half = rows // 2

    @pl.when(head == 0)
    def _():
        cross_ref[...] = lax.dot_general(
            read_ref[...], write_ref[...], (((1,), (1,)), ((), ())),
            preferred_element_type=jnp.float32,
        )
        square_ref[...] = jnp.zeros_like(square_ref)

    cum_column = column_of(cum_table_ref[...], head)
    direct = column_of(gain_ref[...], head)
    incoming = incoming_ref[0]
    for part in range(2):
        here = slice(part * half, (part + 1) * half)
        upto = (part + 1) * half
        x_here = x_ref[here, :]
        row_ids = part * half + lax.broadcasted_iota(jnp.int32, (half, upto), 0)
        column_ids = lax.broadcasted_iota(jnp.int32, (half, upto), 1)
        lower = row_ids >= column_ids
        gap = cum_column[here] - cum_row_ref[0, :, :upto]
        mixing = jnp.where(
            lower,
            jnp.exp(jnp.where(lower, gap, 0.0))
            * cross_ref[here, :upto]
            * size_row_ref[0, :, :upto],
            0.0,
        ).astype(jnp.bfloat16)
        mixed = jnp.dot(mixing, x_ref[:upto, :], preferred_element_type=jnp.float32)
        mixed += jnp.exp(cum_column[here]) * jnp.dot(
            read_ref[here, :], incoming, preferred_element_type=jnp.float32
        )
        mixed += direct * x_here.astype(jnp.float32)
        gate = gate_ref[here, :].astype(jnp.float32)
        gated = mixed * (gate / (1.0 + jnp.exp(-gate)))
        gated_ref[here, :] = gated
        square_ref[here, :] += jnp.sum(gated * gated, axis=1, keepdims=True)


def attention_kernel(group, q_ref, *refs):
    key_refs, value_refs, out_ref = refs[: group + 1], refs[group + 1 : -1], refs[-1]
    rows = q_ref.shape[0]
    half = rows // 2
    position = lax.axis_index("ctx")
    mine = position % group
    has_before = position >= group
    scale = HD ** (-0.5)
    for part in range(2):
        query = q_ref[part * half : (part + 1) * half, :]
        spans = [slice(0, (part + 1) * half)]
        spans += [slice(0, rows)] * (group - 1)
        spans += [slice(part * half, rows)]
        all_scores = []
        for which, span in enumerate(spans):
            scores = lax.dot_general(
                query, key_refs[which][span, :], (((1,), (1,)), ((), ())),
                preferred_element_type=jnp.float32,
            )
            if which == 0 or which == group:
                query_ids = part * half + lax.broadcasted_iota(jnp.int32, scores.shape, 0)
                key_ids = span.start + lax.broadcasted_iota(jnp.int32, scores.shape, 1)
                if which == 0:
                    scores = jnp.where(key_ids <= query_ids, scores, -jnp.inf)
                else:
                    kept = jnp.logical_and(key_ids > query_ids, has_before)
                    scores = jnp.where(kept, scores, -jnp.inf)
            else:
                kept = jnp.logical_or(jnp.bitwise_xor(mine, which) < mine, has_before)
                scores = jnp.where(kept, scores, -jnp.inf)
            all_scores.append(scores)
        maximum = functools.reduce(
            jnp.maximum, [jnp.max(scores, axis=1, keepdims=True) for scores in all_scores]
        )
        total = jnp.zeros_like(maximum)
        attended = jnp.zeros((half, HD), jnp.float32)
        for which, span in enumerate(spans):
            weights = jnp.exp((all_scores[which] - maximum) * scale)
            total += jnp.sum(weights, axis=1, keepdims=True)
            attended += jnp.dot(
                weights.astype(jnp.bfloat16), value_refs[which][span, :],
                preferred_element_type=jnp.float32,
            )
        out_ref[part * half : (part + 1) * half, :] = (attended / total).astype(jnp.bfloat16)


def attend(query, pairs, first_head, heads, group):
    rows = query.shape[0]
    block = (rows, HD)
    return pl.pallas_call(
        functools.partial(attention_kernel, group),
        grid=(heads,),
        in_specs=[pl.BlockSpec(block, lambda h: (0, first_head + h))]
        + [pl.BlockSpec(block, lambda h: (0, h))] * (group + 1)
        + [pl.BlockSpec(block, lambda h: (0, heads + h))] * (group + 1),
        out_specs=pl.BlockSpec(block, lambda h: (0, h)),
        out_shape=jax.ShapeDtypeStruct((rows, heads * HD), jnp.bfloat16),
        compiler_params=pltpu.CompilerParams(vmem_limit_bytes=VMEM_LIMIT),
        cost_estimate=pl.CostEstimate(
            flops=4 * heads * rows * rows * (group + 1) * HD,
            bytes_accessed=2 * heads * rows * HD * (2 * group + 4),
            transcendentals=heads * rows * rows * (group + 1),
        ),
    )(query, *pairs, *pairs)


def per_device(
    space_head_input,
    mixer_gate_input,
    state_write_matrix,
    readout_matrix,
    head_decay_code,
    token_step_code,
    forget_token_code,
    head_direct_gain,
    output_norm_gain,
    attention_query,
    attention_key,
    attention_value,
):
    rows = space_head_input.shape[0]
    local_heads = head_decay_code.shape[0]
    state_size = state_write_matrix.shape[1]
    count = lax.axis_size("ctx")
    position = lax.axis_index("ctx")
    group = WINDOW // rows
    mine = position % group
    shift = lambda value, steps: lax.ppermute(
        value, "ctx", [(source, source + steps) for source in range(count - steps)]
    )
    swap = lambda value, bits: lax.ppermute(
        value, "ctx", [(source, source ^ bits) for source in range(count)]
    )

    sizes, log_decay = decay_factors(
        head_decay_code, token_step_code, forget_token_code, rows * count
    )
    upper = (jnp.arange(rows)[:, None] <= jnp.arange(rows)[None, :]).astype(jnp.float32)
    cumulative = jnp.dot(log_decay, upper, precision=lax.Precision.HIGHEST)
    last = cumulative[:, -1]
    weights = jnp.exp(last[:, None] - cumulative) * sizes

    heads = attention_query.shape[1] // HD
    parts = HEAD_GROUPS if heads % HEAD_GROUPS == 0 else 1
    part_heads = heads // parts
    owns = []
    for part in range(parts):
        columns = slice(part * part_heads * HD, (part + 1) * part_heads * HD)
        owns.append(
            jnp.concatenate([attention_key[:, columns], attention_value[:, columns]], axis=1)
        )
    owns[0], weights = lax.optimization_barrier((owns[0], weights))
    state = pl.pallas_call(
        end_state_kernel,
        grid=(local_heads,),
        in_specs=[
            pl.BlockSpec((rows, P_SIZE), lambda h: (0, h)),
            pl.BlockSpec((rows, state_size), lambda h: (0, 0)),
            pl.BlockSpec((rows, local_heads), lambda h: (0, 0)),
        ],
        out_specs=pl.BlockSpec((1, state_size, P_SIZE), lambda h: (h, 0, 0)),
        out_shape=jax.ShapeDtypeStruct((local_heads, state_size, P_SIZE), jnp.float32),
        cost_estimate=pl.CostEstimate(
            flops=2 * local_heads * rows * state_size * P_SIZE,
            bytes_accessed=2 * local_heads * rows * P_SIZE,
            transcendentals=0,
        ),
    )(space_head_input, state_write_matrix, weights.T)

    def pack(value, log):
        high = log.astype(jnp.bfloat16)
        rest = log - high.astype(jnp.float32)
        middle = rest.astype(jnp.bfloat16)
        low = (rest - middle.astype(jnp.float32)).astype(jnp.bfloat16)
        terms = jnp.stack([high, middle, low], axis=1)[:, :, None]
        extra = jnp.pad(terms, ((0, 0), (0, LOG_ROWS - 3), (0, 0)))
        extra = jnp.broadcast_to(extra, (local_heads, LOG_ROWS, P_SIZE))
        return jnp.concatenate([value.astype(jnp.bfloat16), extra], axis=1)

    def unpack(packed):
        terms = packed[:, state_size : state_size + 3, 0].astype(jnp.float32)
        log = (terms[:, 0] + terms[:, 1]) + terms[:, 2]
        return packed[:, :state_size].astype(jnp.float32), log

    def grown(log):
        return jnp.exp(log)[:, None, None]

    befores = [shift(owns[0], group)]
    gathered = []

    def exchange(part, before, packed):
        sent = {}
        bit = 1
        while bit < group:
            sent[bit] = jnp.where(jnp.bitwise_and(mine, bit) == 0, owns[part], before)
            bit *= 2
        sent, packed = lax.optimization_barrier((sent, packed))
        pairs = [owns[part]]
        for bits in range(1, group):
            top = 1 << (bits.bit_length() - 1)
            pairs.append(swap(sent[top], bits))
        gathered.append(pairs + [before])
        return packed

    prefix = jnp.zeros_like(state)
    prefix_log = jnp.zeros_like(last)
    total = state
    total_log = last
    packed = pack(total, total_log)
    bit = 1
    while bit < group:
        hop = swap(packed, bit)
        if gathered:
            hop, gathered[-1] = lax.optimization_barrier((hop, gathered[-1]))
        other, other_log = unpack(hop)
        later = jnp.bitwise_and(position, bit) != 0
        prefix = jnp.where(later, prefix + grown(prefix_log) * other, prefix)
        prefix_log = jnp.where(later, prefix_log + other_log, prefix_log)
        total = jnp.where(
            later, total + grown(total_log) * other, other + grown(other_log) * total
        )
        total_log = total_log + other_log
        packed = pack(total, total_log)
        done = len(gathered)
        if done < parts:
            before, packed = lax.optimization_barrier((befores[done], packed))
            if done + 1 < parts:
                owns[done + 1], before = lax.optimization_barrier((owns[done + 1], before))
                befores.append(shift(owns[done + 1], group))
            packed = exchange(done, before, packed)
        bit *= 2
    while len(gathered) < parts:
        done = len(gathered)
        if done + 1 < parts:
            befores.append(shift(owns[done + 1], group))
        packed = exchange(done, befores[done], packed)
    earlier, earlier_log = unpack(shift(packed, group))
    span = 1
    while span * group < count - group:
        more, more_log = unpack(shift(pack(earlier, earlier_log), span * group))
        earlier = earlier + grown(earlier_log) * more
        earlier_log = earlier_log + more_log
        span *= 2
    incoming = (prefix + grown(prefix_log) * earlier).astype(jnp.bfloat16)

    gated, squares = pl.pallas_call(
        mixer_kernel,
        grid=(local_heads,),
        in_specs=[
            pl.BlockSpec((rows, P_SIZE), lambda h: (0, h)),
            pl.BlockSpec((rows, P_SIZE), lambda h: (0, h)),
            pl.BlockSpec((rows, state_size), lambda h: (0, 0)),
            pl.BlockSpec((rows, state_size), lambda h: (0, 0)),
            pl.BlockSpec((1, 1, rows), lambda h: (h, 0, 0)),
            pl.BlockSpec((1, 1, rows), lambda h: (h, 0, 0)),
            pl.BlockSpec((rows, local_heads), lambda h: (0, 0)),
            pl.BlockSpec((1, local_heads), lambda h: (0, 0)),
            pl.BlockSpec((1, state_size, P_SIZE), lambda h: (h, 0, 0)),
        ],
        out_specs=[
            pl.BlockSpec((rows, P_SIZE), lambda h: (0, h)),
            pl.BlockSpec((rows, 1), lambda h: (0, 0)),
        ],
        out_shape=[
            jax.ShapeDtypeStruct((rows, local_heads * P_SIZE), jnp.float32),
            jax.ShapeDtypeStruct((rows, 1), jnp.float32),
        ],
        scratch_shapes=[pltpu.VMEM((rows, rows), jnp.float32)],
        compiler_params=pltpu.CompilerParams(vmem_limit_bytes=VMEM_LIMIT),
        cost_estimate=pl.CostEstimate(
            flops=2 * local_heads * rows * (rows + state_size) * P_SIZE,
            bytes_accessed=8 * local_heads * rows * P_SIZE,
            transcendentals=local_heads * rows * (rows + P_SIZE),
        ),
    )(
        space_head_input,
        mixer_gate_input,
        state_write_matrix,
        readout_matrix,
        cumulative[:, None, :],
        sizes[:, None, :],
        cumulative.T,
        head_direct_gain[None, :],
        incoming,
    )
    squares = lax.psum(squares[:, 0], "head")
    mixer_out = (
        gated * lax.rsqrt(squares[:, None] / (SSM_HEADS * P_SIZE) + 1e-05) * output_norm_gain
    ).astype(jnp.bfloat16)

    outs = [
        attend(attention_query, gathered[part], part * part_heads, part_heads, group)
        for part in range(parts)
    ]
    window_out = outs[0] if parts == 1 else jnp.concatenate(outs, axis=1)
    return (mixer_out, window_out)


def solution(mesh):
    return jax.shard_map(
        per_device,
        mesh=mesh,
        in_specs=(
            P("ctx", "head"),
            P("ctx", "head"),
            P("ctx", None),
            P("ctx", None),
            P("head"),
            P("head", "ctx"),
            P("ctx"),
            P("head"),
            P("head"),
            P("ctx", "head"),
            P("ctx", "head"),
            P("ctx", "head"),
        ),
        out_specs=(P("ctx", "head"), P("ctx", "head")),
        check_vma=False,
    )
```

```python
import functools
import math

import jax
import jax.numpy as jnp
from jax import lax
from jax.experimental import pallas as pl
from jax.experimental.pallas import tpu as pltpu
from jax.sharding import PartitionSpec as P

HD = 128
SSM_HEADS = 24
P_SIZE = 256
WINDOW = 2048
HEAD_GROUPS = 2
LOG_ROWS = 16
VMEM_LIMIT = 48 * 1024 * 1024


def head_rates(head_decay_code, token_total_count):
    level_count = head_decay_code.astype(jnp.float32)
    quick_log = math.log(0.03) - level_count / 4.0 * math.log(0.03 * token_total_count)
    gentle = -math.log(token_total_count) - (level_count - 4.0) / 3.0 * math.log(4.0)
    return jnp.exp(jnp.where(level_count <= 4.0, quick_log, gentle))


def decay_factors(head_decay_code, token_step_code, forget_token_code, token_total_count):
    every_rate = head_rates(head_decay_code, token_total_count)
    token_step_sizes = jnp.sqrt(2.0 * every_rate)[:, None] * jnp.exp(
        math.log(2.0) * (0.5 * token_step_code.astype(jnp.float32) - 0.75)
    )
    logarithm_decay = (
        -jnp.sqrt(0.5 * every_rate)[:, None] * token_step_sizes
        - 0.2 * forget_token_code.astype(jnp.float32)[None, :]
    )
    return (token_step_sizes, logarithm_decay)


def column_of(table, index):
    lanes = lax.broadcasted_iota(jnp.int32, table.shape, 1)
    return jnp.sum(jnp.where(lanes == index, table, 0.0), axis=1, keepdims=True)


def end_state_kernel(x_ref, write_ref, weight_ref, state_ref):
    weight = column_of(weight_ref[...], pl.program_id(0))
    weighted = (write_ref[...].astype(jnp.float32) * weight).astype(jnp.bfloat16)
    state_ref[0] = lax.dot_general(
        weighted, x_ref[...], (((0,), (0,)), ((), ())), preferred_element_type=jnp.float32
    )


def mixer_kernel(
    x_ref, gate_ref, write_ref, read_ref, cum_row_ref, size_row_ref, cum_table_ref, gain_ref,
    incoming_ref, gated_ref, square_ref, cross_ref,
):
    head = pl.program_id(0)
    rows = x_ref.shape[0]
    half = rows // 2

    @pl.when(head == 0)
    def _():
        cross_ref[...] = lax.dot_general(
            read_ref[...], write_ref[...], (((1,), (1,)), ((), ())),
            preferred_element_type=jnp.float32,
        )
        square_ref[...] = jnp.zeros_like(square_ref)

    cum_column = column_of(cum_table_ref[...], head)
    direct = column_of(gain_ref[...], head)
    incoming = incoming_ref[0]
    for part in range(2):
        here = slice(part * half, (part + 1) * half)
        upto = (part + 1) * half
        x_here = x_ref[here, :]
        row_ids = part * half + lax.broadcasted_iota(jnp.int32, (half, upto), 0)
        column_ids = lax.broadcasted_iota(jnp.int32, (half, upto), 1)
        lower = row_ids >= column_ids
        gap = cum_column[here] - cum_row_ref[0, :, :upto]
        mixing = jnp.where(
            lower,
            jnp.exp(jnp.where(lower, gap, 0.0))
            * cross_ref[here, :upto]
            * size_row_ref[0, :, :upto],
            0.0,
        ).astype(jnp.bfloat16)
        mixed = jnp.dot(mixing, x_ref[:upto, :], preferred_element_type=jnp.float32)
        mixed += jnp.exp(cum_column[here]) * jnp.dot(
            read_ref[here, :], incoming, preferred_element_type=jnp.float32
        )
        mixed += direct * x_here.astype(jnp.float32)
        gate = gate_ref[here, :].astype(jnp.float32)
        gated = mixed * (gate / (1.0 + jnp.exp(-gate)))
        gated_ref[here, :] = gated
        square_ref[here, :] += jnp.sum(gated * gated, axis=1, keepdims=True)


def attention_kernel(group, q_ref, *refs):
    key_refs, value_refs, out_ref = refs[: group + 1], refs[group + 1 : -1], refs[-1]
    rows = q_ref.shape[0]
    half = rows // 2
    position = lax.axis_index("ctx")
    mine = position % group
    has_before = position >= group
    scale = HD ** (-0.5)
    for part in range(2):
        query = q_ref[part * half : (part + 1) * half, :]
        spans = [slice(0, (part + 1) * half)]
        spans += [slice(0, rows)] * (group - 1)
        spans += [slice(part * half, rows)]
        all_scores = []
        for which, span in enumerate(spans):
            scores = lax.dot_general(
                query, key_refs[which][span, :], (((1,), (1,)), ((), ())),
                preferred_element_type=jnp.float32,
            )
            if which == 0 or which == group:
                query_ids = part * half + lax.broadcasted_iota(jnp.int32, scores.shape, 0)
                key_ids = span.start + lax.broadcasted_iota(jnp.int32, scores.shape, 1)
                if which == 0:
                    scores = jnp.where(key_ids <= query_ids, scores, -jnp.inf)
                else:
                    kept = jnp.logical_and(key_ids > query_ids, has_before)
                    scores = jnp.where(kept, scores, -jnp.inf)
            else:
                kept = jnp.logical_or(jnp.bitwise_xor(mine, which) < mine, has_before)
                scores = jnp.where(kept, scores, -jnp.inf)
            all_scores.append(scores)
        maximum = functools.reduce(
            jnp.maximum, [jnp.max(scores, axis=1, keepdims=True) for scores in all_scores]
        )
        total = jnp.zeros_like(maximum)
        attended = jnp.zeros((half, HD), jnp.float32)
        for which, span in enumerate(spans):
            weights = jnp.exp((all_scores[which] - maximum) * scale)
            total += jnp.sum(weights, axis=1, keepdims=True)
            attended += jnp.dot(
                weights.astype(jnp.bfloat16), value_refs[which][span, :],
                preferred_element_type=jnp.float32,
            )
        out_ref[part * half : (part + 1) * half, :] = (attended / total).astype(jnp.bfloat16)


def attend(query, pairs, first_head, heads, group):
    rows = query.shape[0]
    block = (rows, HD)
    return pl.pallas_call(
        functools.partial(attention_kernel, group),
        grid=(heads,),
        in_specs=[pl.BlockSpec(block, lambda h: (0, first_head + h))]
        + [pl.BlockSpec(block, lambda h: (0, h))] * (group + 1)
        + [pl.BlockSpec(block, lambda h: (0, heads + h))] * (group + 1),
        out_specs=pl.BlockSpec(block, lambda h: (0, h)),
        out_shape=jax.ShapeDtypeStruct((rows, heads * HD), jnp.bfloat16),
        compiler_params=pltpu.CompilerParams(vmem_limit_bytes=VMEM_LIMIT),
        cost_estimate=pl.CostEstimate(
            flops=4 * heads * rows * rows * (group + 1) * HD,
            bytes_accessed=2 * heads * rows * HD * (2 * group + 4),
            transcendentals=heads * rows * rows * (group + 1),
        ),
    )(query, *pairs, *pairs)


def per_device(
    space_head_input,
    mixer_gate_input,
    state_write_matrix,
    readout_matrix,
    head_decay_code,
    token_step_code,
    forget_token_code,
    head_direct_gain,
    output_norm_gain,
    attention_query,
    attention_key,
    attention_value,
):
    rows = space_head_input.shape[0]
    local_heads = head_decay_code.shape[0]
    state_size = state_write_matrix.shape[1]
    count = lax.axis_size("ctx")
    position = lax.axis_index("ctx")
    group = WINDOW // rows
    mine = position % group
    shift = lambda value, steps: lax.ppermute(
        value, "ctx", [(source, source + steps) for source in range(count - steps)]
    )
    swap = lambda value, bits: lax.ppermute(
        value, "ctx", [(source, source ^ bits) for source in range(count)]
    )

    sizes, log_decay = decay_factors(
        head_decay_code, token_step_code, forget_token_code, rows * count
    )
    upper = (jnp.arange(rows)[:, None] <= jnp.arange(rows)[None, :]).astype(jnp.float32)
    cumulative = jnp.dot(log_decay, upper, precision=lax.Precision.HIGHEST)
    last = cumulative[:, -1]
    weights = jnp.exp(last[:, None] - cumulative) * sizes

    heads = attention_query.shape[1] // HD
    parts = HEAD_GROUPS if heads % HEAD_GROUPS == 0 else 1
    part_heads = heads // parts
    owns = []
    for part in range(parts):
        columns = slice(part * part_heads * HD, (part + 1) * part_heads * HD)
        owns.append(
            jnp.concatenate([attention_key[:, columns], attention_value[:, columns]], axis=1)
        )
    owns[0], weights = lax.optimization_barrier((owns[0], weights))
    state = pl.pallas_call(
        end_state_kernel,
        grid=(local_heads,),
        in_specs=[
            pl.BlockSpec((rows, P_SIZE), lambda h: (0, h)),
            pl.BlockSpec((rows, state_size), lambda h: (0, 0)),
            pl.BlockSpec((rows, local_heads), lambda h: (0, 0)),
        ],
        out_specs=pl.BlockSpec((1, state_size, P_SIZE), lambda h: (h, 0, 0)),
        out_shape=jax.ShapeDtypeStruct((local_heads, state_size, P_SIZE), jnp.float32),
        cost_estimate=pl.CostEstimate(
            flops=2 * local_heads * rows * state_size * P_SIZE,
            bytes_accessed=2 * local_heads * rows * P_SIZE,
            transcendentals=0,
        ),
    )(space_head_input, state_write_matrix, weights.T)

    def pack(value, log):
        high = log.astype(jnp.bfloat16)
        rest = log - high.astype(jnp.float32)
        middle = rest.astype(jnp.bfloat16)
        low = (rest - middle.astype(jnp.float32)).astype(jnp.bfloat16)
        terms = jnp.stack([high, middle, low], axis=1)[:, :, None]
        extra = jnp.pad(terms, ((0, 0), (0, LOG_ROWS - 3), (0, 0)))
        extra = jnp.broadcast_to(extra, (local_heads, LOG_ROWS, P_SIZE))
        return jnp.concatenate([value.astype(jnp.bfloat16), extra], axis=1)

    def unpack(packed):
        terms = packed[:, state_size : state_size + 3, 0].astype(jnp.float32)
        log = (terms[:, 0] + terms[:, 1]) + terms[:, 2]
        return packed[:, :state_size].astype(jnp.float32), log

    def grown(log):
        return jnp.exp(log)[:, None, None]

    def half_swap(value, bits, forward):
        return lax.ppermute(
            value,
            "ctx",
            [
                (source, source ^ bits)
                for source in range(count)
                if (source < source ^ bits) == forward
            ],
        )

    def both_ways(value, forward):
        return [half_swap(value, bits, forward) for bits in range(1, group)]

    befores = [shift(owns[0], group)]
    own_hops = []
    before_hops = []

    prefix = jnp.zeros_like(state)
    prefix_log = jnp.zeros_like(last)
    total = state
    total_log = last
    packed = pack(total, total_log)
    bit = 1
    while bit < group:
        if bit == 1:
            own_hops.append(both_ways(owns[0], True))
        hop = swap(packed, bit)
        if bit > 1:
            hop, own_hops[0] = lax.optimization_barrier((hop, own_hops[0]))
        other, other_log = unpack(hop)
        later = jnp.bitwise_and(position, bit) != 0
        prefix = jnp.where(later, prefix + grown(prefix_log) * other, prefix)
        prefix_log = jnp.where(later, prefix_log + other_log, prefix_log)
        total = jnp.where(
            later, total + grown(total_log) * other, other + grown(other_log) * total
        )
        total_log = total_log + other_log
        packed = pack(total, total_log)
        if bit == 1:
            befores[0], packed = lax.optimization_barrier((befores[0], packed))
            if parts > 1:
                owns[1], packed = lax.optimization_barrier((owns[1], packed))
                befores.append(shift(owns[1], group))
            before_hops.append(both_ways(befores[0], False))
        elif parts > 1 and len(own_hops) == 1:
            befores[1], owns[1], packed = lax.optimization_barrier((befores[1], owns[1], packed))
            own_hops.append(both_ways(owns[1], True))
            before_hops.append(both_ways(befores[1], False))
        bit *= 2
    hop = shift(packed, group)
    hop, before_hops[0] = lax.optimization_barrier((hop, before_hops[0]))
    earlier, earlier_log = unpack(hop)
    span = 1
    while span * group < count - group:
        hop = shift(pack(earlier, earlier_log), span * group)
        if span == 1 and parts > 1:
            hop, own_hops[1] = lax.optimization_barrier((hop, own_hops[1]))
        more, more_log = unpack(hop)
        earlier = earlier + grown(earlier_log) * more
        earlier_log = earlier_log + more_log
        span *= 2
    incoming = (prefix + grown(prefix_log) * earlier).astype(jnp.bfloat16)

    gathered = []
    for part in range(parts):
        pairs = [owns[part]]
        for bits in range(1, group):
            from_earlier = jnp.bitwise_xor(mine, bits) < mine
            pairs.append(
                jnp.where(from_earlier, own_hops[part][bits - 1], before_hops[part][bits - 1])
            )
        gathered.append(pairs + [befores[part]])

    gated, squares = pl.pallas_call(
        mixer_kernel,
        grid=(local_heads,),
        in_specs=[
            pl.BlockSpec((rows, P_SIZE), lambda h: (0, h)),
            pl.BlockSpec((rows, P_SIZE), lambda h: (0, h)),
            pl.BlockSpec((rows, state_size), lambda h: (0, 0)),
            pl.BlockSpec((rows, state_size), lambda h: (0, 0)),
            pl.BlockSpec((1, 1, rows), lambda h: (h, 0, 0)),
            pl.BlockSpec((1, 1, rows), lambda h: (h, 0, 0)),
            pl.BlockSpec((rows, local_heads), lambda h: (0, 0)),
            pl.BlockSpec((1, local_heads), lambda h: (0, 0)),
            pl.BlockSpec((1, state_size, P_SIZE), lambda h: (h, 0, 0)),
        ],
        out_specs=[
            pl.BlockSpec((rows, P_SIZE), lambda h: (0, h)),
            pl.BlockSpec((rows, 1), lambda h: (0, 0)),
        ],
        out_shape=[
            jax.ShapeDtypeStruct((rows, local_heads * P_SIZE), jnp.float32),
            jax.ShapeDtypeStruct((rows, 1), jnp.float32),
        ],
        scratch_shapes=[pltpu.VMEM((rows, rows), jnp.float32)],
        compiler_params=pltpu.CompilerParams(vmem_limit_bytes=VMEM_LIMIT),
        cost_estimate=pl.CostEstimate(
            flops=2 * local_heads * rows * (rows + state_size) * P_SIZE,
            bytes_accessed=8 * local_heads * rows * P_SIZE,
            transcendentals=local_heads * rows * (rows + P_SIZE),
        ),
    )(
        space_head_input,
        mixer_gate_input,
        state_write_matrix,
        readout_matrix,
        cumulative[:, None, :],
        sizes[:, None, :],
        cumulative.T,
        head_direct_gain[None, :],
        incoming,
    )
    squares = lax.psum(squares[:, 0], "head")
    mixer_out = (
        gated * lax.rsqrt(squares[:, None] / (SSM_HEADS * P_SIZE) + 1e-05) * output_norm_gain
    ).astype(jnp.bfloat16)

    outs = [
        attend(attention_query, gathered[part], part * part_heads, part_heads, group)
        for part in range(parts)
    ]
    window_out = outs[0] if parts == 1 else jnp.concatenate(outs, axis=1)
    return (mixer_out, window_out)


def solution(mesh):
    return jax.shard_map(
        per_device,
        mesh=mesh,
        in_specs=(
            P("ctx", "head"),
            P("ctx", "head"),
            P("ctx", None),
            P("ctx", None),
            P("head"),
            P("head", "ctx"),
            P("ctx"),
            P("head"),
            P("head"),
            P("ctx", "head"),
            P("ctx", "head"),
            P("ctx", "head"),
        ),
        out_specs=(P("ctx", "head"), P("ctx", "head")),
        check_vma=False,
    )
```

```python
import functools
import math

import jax
import jax.numpy as jnp
from jax import lax
from jax.experimental import pallas as pl
from jax.experimental.pallas import tpu as pltpu
from jax.sharding import PartitionSpec as P

HD = 128
SSM_HEADS = 24
P_SIZE = 256
WINDOW = 2048
HEAD_GROUPS = 2
LOG_ROWS = 16
VMEM_LIMIT = 48 * 1024 * 1024


def head_rates(head_decay_code, token_total_count):
    level_count = head_decay_code.astype(jnp.float32)
    quick_log = math.log(0.03) - level_count / 4.0 * math.log(0.03 * token_total_count)
    gentle = -math.log(token_total_count) - (level_count - 4.0) / 3.0 * math.log(4.0)
    return jnp.exp(jnp.where(level_count <= 4.0, quick_log, gentle))


def decay_factors(head_decay_code, token_step_code, forget_token_code, token_total_count):
    every_rate = head_rates(head_decay_code, token_total_count)
    token_step_sizes = jnp.sqrt(2.0 * every_rate)[:, None] * jnp.exp(
        math.log(2.0) * (0.5 * token_step_code.astype(jnp.float32) - 0.75)
    )
    logarithm_decay = (
        -jnp.sqrt(0.5 * every_rate)[:, None] * token_step_sizes
        - 0.2 * forget_token_code.astype(jnp.float32)[None, :]
    )
    return (token_step_sizes, logarithm_decay)


def column_of(table, index):
    lanes = lax.broadcasted_iota(jnp.int32, table.shape, 1)
    return jnp.sum(jnp.where(lanes == index, table, 0.0), axis=1, keepdims=True)


def end_state_kernel(x_ref, write_ref, weight_ref, state_ref):
    weight = column_of(weight_ref[...], pl.program_id(0))
    weighted = (write_ref[...].astype(jnp.float32) * weight).astype(jnp.bfloat16)
    state_ref[0] = lax.dot_general(
        weighted, x_ref[...], (((0,), (0,)), ((), ())), preferred_element_type=jnp.float32
    )


def mixer_kernel(
    x_ref, gate_ref, write_ref, read_ref, cum_row_ref, size_row_ref, cum_table_ref, gain_ref,
    incoming_ref, gated_ref, square_ref, cross_ref,
):
    head = pl.program_id(0)
    rows = x_ref.shape[0]
    half = rows // 2

    @pl.when(head == 0)
    def _():
        cross_ref[...] = lax.dot_general(
            read_ref[...], write_ref[...], (((1,), (1,)), ((), ())),
            preferred_element_type=jnp.float32,
        )
        square_ref[...] = jnp.zeros_like(square_ref)

    cum_column = column_of(cum_table_ref[...], head)
    direct = column_of(gain_ref[...], head)
    incoming = incoming_ref[0]
    for part in range(2):
        here = slice(part * half, (part + 1) * half)
        upto = (part + 1) * half
        x_here = x_ref[here, :]
        row_ids = part * half + lax.broadcasted_iota(jnp.int32, (half, upto), 0)
        column_ids = lax.broadcasted_iota(jnp.int32, (half, upto), 1)
        lower = row_ids >= column_ids
        gap = cum_column[here] - cum_row_ref[0, :, :upto]
        mixing = jnp.where(
            lower,
            jnp.exp(jnp.where(lower, gap, 0.0))
            * cross_ref[here, :upto]
            * size_row_ref[0, :, :upto],
            0.0,
        ).astype(jnp.bfloat16)
        mixed = jnp.dot(mixing, x_ref[:upto, :], preferred_element_type=jnp.float32)
        mixed += jnp.exp(cum_column[here]) * jnp.dot(
            read_ref[here, :], incoming, preferred_element_type=jnp.float32
        )
        mixed += direct * x_here.astype(jnp.float32)
        gate = gate_ref[here, :].astype(jnp.float32)
        gated = mixed * (gate / (1.0 + jnp.exp(-gate)))
        gated_ref[here, :] = gated
        square_ref[here, :] += jnp.sum(gated * gated, axis=1, keepdims=True)


def attention_kernel(group, q_ref, *refs):
    key_refs, value_refs, out_ref = refs[: group + 1], refs[group + 1 : -1], refs[-1]
    rows = q_ref.shape[0]
    half = rows // 2
    position = lax.axis_index("ctx")
    mine = position % group
    has_before = position >= group
    scale = HD ** (-0.5)
    for part in range(2):
        query = q_ref[part * half : (part + 1) * half, :]
        spans = [slice(0, (part + 1) * half)]
        spans += [slice(0, rows)] * (group - 1)
        spans += [slice(part * half, rows)]
        all_scores = []
        for which, span in enumerate(spans):
            scores = lax.dot_general(
                query, key_refs[which][span, :], (((1,), (1,)), ((), ())),
                preferred_element_type=jnp.float32,
            )
            if which == 0 or which == group:
                query_ids = part * half + lax.broadcasted_iota(jnp.int32, scores.shape, 0)
                key_ids = span.start + lax.broadcasted_iota(jnp.int32, scores.shape, 1)
                if which == 0:
                    scores = jnp.where(key_ids <= query_ids, scores, -jnp.inf)
                else:
                    kept = jnp.logical_and(key_ids > query_ids, has_before)
                    scores = jnp.where(kept, scores, -jnp.inf)
            else:
                kept = jnp.logical_or(jnp.bitwise_xor(mine, which) < mine, has_before)
                scores = jnp.where(kept, scores, -jnp.inf)
            all_scores.append(scores)
        maximum = functools.reduce(
            jnp.maximum, [jnp.max(scores, axis=1, keepdims=True) for scores in all_scores]
        )
        total = jnp.zeros_like(maximum)
        attended = jnp.zeros((half, HD), jnp.float32)
        for which, span in enumerate(spans):
            weights = jnp.exp((all_scores[which] - maximum) * scale)
            total += jnp.sum(weights, axis=1, keepdims=True)
            attended += jnp.dot(
                weights.astype(jnp.bfloat16), value_refs[which][span, :],
                preferred_element_type=jnp.float32,
            )
        out_ref[part * half : (part + 1) * half, :] = (attended / total).astype(jnp.bfloat16)


def attend(query, pairs, first_head, heads, group):
    rows = query.shape[0]
    block = (rows, HD)
    return pl.pallas_call(
        functools.partial(attention_kernel, group),
        grid=(heads,),
        in_specs=[pl.BlockSpec(block, lambda h: (0, first_head + h))]
        + [pl.BlockSpec(block, lambda h: (0, h))] * (group + 1)
        + [pl.BlockSpec(block, lambda h: (0, heads + h))] * (group + 1),
        out_specs=pl.BlockSpec(block, lambda h: (0, h)),
        out_shape=jax.ShapeDtypeStruct((rows, heads * HD), jnp.bfloat16),
        compiler_params=pltpu.CompilerParams(vmem_limit_bytes=VMEM_LIMIT),
        cost_estimate=pl.CostEstimate(flops=1, bytes_accessed=1, transcendentals=0),
    )(query, *pairs, *pairs)


def per_device(
    space_head_input,
    mixer_gate_input,
    state_write_matrix,
    readout_matrix,
    head_decay_code,
    token_step_code,
    forget_token_code,
    head_direct_gain,
    output_norm_gain,
    attention_query,
    attention_key,
    attention_value,
):
    rows = space_head_input.shape[0]
    local_heads = head_decay_code.shape[0]
    state_size = state_write_matrix.shape[1]
    count = lax.axis_size("ctx")
    position = lax.axis_index("ctx")
    group = WINDOW // rows
    mine = position % group
    shift = lambda value, steps: lax.ppermute(
        value, "ctx", [(source, source + steps) for source in range(count - steps)]
    )
    swap = lambda value, bits: lax.ppermute(
        value, "ctx", [(source, source ^ bits) for source in range(count)]
    )

    sizes, log_decay = decay_factors(
        head_decay_code, token_step_code, forget_token_code, rows * count
    )
    upper = (jnp.arange(rows)[:, None] <= jnp.arange(rows)[None, :]).astype(jnp.float32)
    cumulative = jnp.dot(log_decay, upper, precision=lax.Precision.HIGHEST)
    last = cumulative[:, -1]
    weights = jnp.exp(last[:, None] - cumulative) * sizes

    heads = attention_query.shape[1] // HD
    parts = HEAD_GROUPS if heads % HEAD_GROUPS == 0 else 1
    part_heads = heads // parts
    owns = []
    for part in range(parts):
        columns = slice(part * part_heads * HD, (part + 1) * part_heads * HD)
        owns.append(
            jnp.concatenate([attention_key[:, columns], attention_value[:, columns]], axis=1)
        )
    owns[0], weights = lax.optimization_barrier((owns[0], weights))
    state = pl.pallas_call(
        end_state_kernel,
        grid=(local_heads,),
        in_specs=[
            pl.BlockSpec((rows, P_SIZE), lambda h: (0, h)),
            pl.BlockSpec((rows, state_size), lambda h: (0, 0)),
            pl.BlockSpec((rows, local_heads), lambda h: (0, 0)),
        ],
        out_specs=pl.BlockSpec((1, state_size, P_SIZE), lambda h: (h, 0, 0)),
        out_shape=jax.ShapeDtypeStruct((local_heads, state_size, P_SIZE), jnp.float32),
        cost_estimate=pl.CostEstimate(flops=1, bytes_accessed=1, transcendentals=0),
    )(space_head_input, state_write_matrix, weights.T)

    def pack(value, log):
        high = log.astype(jnp.bfloat16)
        rest = log - high.astype(jnp.float32)
        middle = rest.astype(jnp.bfloat16)
        low = (rest - middle.astype(jnp.float32)).astype(jnp.bfloat16)
        terms = jnp.stack([high, middle, low], axis=1)[:, :, None]
        extra = jnp.pad(terms, ((0, 0), (0, LOG_ROWS - 3), (0, 0)))
        extra = jnp.broadcast_to(extra, (local_heads, LOG_ROWS, P_SIZE))
        return jnp.concatenate([value.astype(jnp.bfloat16), extra], axis=1)

    def unpack(packed):
        terms = packed[:, state_size : state_size + 3, 0].astype(jnp.float32)
        log = (terms[:, 0] + terms[:, 1]) + terms[:, 2]
        return packed[:, :state_size].astype(jnp.float32), log

    def grown(log):
        return jnp.exp(log)[:, None, None]

    befores = [shift(owns[0], group)]
    gathered = []

    def exchange(part, before, packed):
        sent = {}
        bit = 1
        while bit < group:
            sent[bit] = jnp.where(jnp.bitwise_and(mine, bit) == 0, owns[part], before)
            bit *= 2
        sent, packed = lax.optimization_barrier((sent, packed))
        pairs = [owns[part]]
        for bits in range(1, group):
            top = 1 << (bits.bit_length() - 1)
            pairs.append(swap(sent[top], bits))
        gathered.append(pairs + [before])
        return packed

    prefix = jnp.zeros_like(state)
    prefix_log = jnp.zeros_like(last)
    total = state
    total_log = last
    packed = pack(total, total_log)
    bit = 1
    while bit < group:
        hop = swap(packed, bit)
        if gathered:
            hop, gathered[-1] = lax.optimization_barrier((hop, gathered[-1]))
        other, other_log = unpack(hop)
        later = jnp.bitwise_and(position, bit) != 0
        prefix = jnp.where(later, prefix + grown(prefix_log) * other, prefix)
        prefix_log = jnp.where(later, prefix_log + other_log, prefix_log)
        total = jnp.where(
            later, total + grown(total_log) * other, other + grown(other_log) * total
        )
        total_log = total_log + other_log
        packed = pack(total, total_log)
        done = len(gathered)
        if done < parts:
            before, packed = lax.optimization_barrier((befores[done], packed))
            if done + 1 < parts:
                owns[done + 1], before = lax.optimization_barrier((owns[done + 1], before))
                befores.append(shift(owns[done + 1], group))
            packed = exchange(done, before, packed)
        bit *= 2
    while len(gathered) < parts:
        done = len(gathered)
        if done + 1 < parts:
            befores.append(shift(owns[done + 1], group))
        packed = exchange(done, befores[done], packed)
    hop = shift(packed, group)
    hop, gathered[-1][1 : group - 1] = lax.optimization_barrier(
        (hop, gathered[-1][1 : group - 1])
    )
    earlier, earlier_log = unpack(hop)
    span = 1
    while span * group < count - group:
        more, more_log = unpack(shift(pack(earlier, earlier_log), span * group))
        earlier = earlier + grown(earlier_log) * more
        earlier_log = earlier_log + more_log
        span *= 2
    incoming = (prefix + grown(prefix_log) * earlier).astype(jnp.bfloat16)

    gated, squares = pl.pallas_call(
        mixer_kernel,
        grid=(local_heads,),
        in_specs=[
            pl.BlockSpec((rows, P_SIZE), lambda h: (0, h)),
            pl.BlockSpec((rows, P_SIZE), lambda h: (0, h)),
            pl.BlockSpec((rows, state_size), lambda h: (0, 0)),
            pl.BlockSpec((rows, state_size), lambda h: (0, 0)),
            pl.BlockSpec((1, 1, rows), lambda h: (h, 0, 0)),
            pl.BlockSpec((1, 1, rows), lambda h: (h, 0, 0)),
            pl.BlockSpec((rows, local_heads), lambda h: (0, 0)),
            pl.BlockSpec((1, local_heads), lambda h: (0, 0)),
            pl.BlockSpec((1, state_size, P_SIZE), lambda h: (h, 0, 0)),
        ],
        out_specs=[
            pl.BlockSpec((rows, P_SIZE), lambda h: (0, h)),
            pl.BlockSpec((rows, 1), lambda h: (0, 0)),
        ],
        out_shape=[
            jax.ShapeDtypeStruct((rows, local_heads * P_SIZE), jnp.float32),
            jax.ShapeDtypeStruct((rows, 1), jnp.float32),
        ],
        scratch_shapes=[pltpu.VMEM((rows, rows), jnp.float32)],
        compiler_params=pltpu.CompilerParams(vmem_limit_bytes=VMEM_LIMIT),
        cost_estimate=pl.CostEstimate(flops=1, bytes_accessed=1, transcendentals=0),
    )(
        space_head_input,
        mixer_gate_input,
        state_write_matrix,
        readout_matrix,
        cumulative[:, None, :],
        sizes[:, None, :],
        cumulative.T,
        head_direct_gain[None, :],
        incoming,
    )
    squares = lax.psum(squares[:, 0], "head")
    mixer_out = (
        gated * lax.rsqrt(squares[:, None] / (SSM_HEADS * P_SIZE) + 1e-05) * output_norm_gain
    ).astype(jnp.bfloat16)

    mixer_out, late_query = lax.optimization_barrier((mixer_out, attention_query))
    outs = []
    for part in range(parts):
        query = attention_query if part + 1 < parts else late_query
        outs.append(attend(query, gathered[part], part * part_heads, part_heads, group))
    window_out = outs[0] if parts == 1 else jnp.concatenate(outs, axis=1)
    return (mixer_out, window_out)


def solution(mesh):
    return jax.shard_map(
        per_device,
        mesh=mesh,
        in_specs=(
            P("ctx", "head"),
            P("ctx", "head"),
            P("ctx", None),
            P("ctx", None),
            P("head"),
            P("head", "ctx"),
            P("ctx"),
            P("head"),
            P("head"),
            P("ctx", "head"),
            P("ctx", "head"),
            P("ctx", "head"),
        ),
        out_specs=(P("ctx", "head"), P("ctx", "head")),
        check_vma=False,
    )
```
